32 devices in a mesh: dp: 8 (over z, y), sp: 4 (over x, core).
Axes of the slice: x: 2, y: 2, z: 4, core: 2. Of those that a mesh axis runs over, the one named last changes fastest.
Arguments:
- normed: bfloat16 [4096, 2560], P(('dp', 'sp')), may hold values from -6 to 6
- w_query: bfloat16 [2560, 4096], P(None, 'sp'), may hold values from -0.125 to 0.125
- key_weight: bfloat16 [2560, 512], P(None, 'sp'), may hold values from -0.125 to 0.125
- value_weight: bfloat16 [2560, 512], P(None, 'sp'), may hold values from -0.125 to 0.125
- q_gain: float32 [128], replicated, may hold values from 0.25 to 1.75
- key_norm_gain: float32 [128], replicated, may hold values from 0.25 to 1.75
- ctx_grad: bfloat16 [4096, 4096], P(('dp', 'sp')), may hold values from -6 to 6
- lengths: int32 [8], P('dp'), may hold values from 64 to 512, as said below
Outputs:
- normed_input_gradient: bfloat16 [4096, 2560], P(('dp', 'sp'))
- grad_w_query: float32 [2560, 4096], P('dp', 'sp')
- grad_w_key: float32 [2560, 512], P('dp', 'sp')
- grad_w_value: float32 [2560, 512], P('dp', 'sp')
The draws below stay inside these ranges and needn't reach their ends.
Inputs may be any that keep to these rules, and one draw needn't show every extreme that they name: `lengths`: in every draw some response has its whole span valid and some only one eighth of 512.
All inputs are finite; a program needn't handle non-finite values.
Results may differ from the reference program's by a relative error of at most 0.008.
Values may be sent and summed in bfloat16 or wider, within the bound.
No kernel may reach another device: no remote copies, remote signals or barrier semaphores. Data moves between devices by JAX's collectives and lax.ppermute only.
A program may use at most 128 MiB of HBM per device.

```python
import math
import jax
import jax.numpy as jnp
from jax import lax

INPUT_FEATURES = 2560
QUERY_HEADS = 32
KEY_HEADS = 4
HEAD_SIZE = 128
QUERY_PER_KV = 8
SPAN_TOKENS = 512
RESPONSES = 8
TOKENS = 4096


def draw_lengths(key, part):
    key = jax.random.fold_in(key, 11)
    first_key, second_key = jax.random.split(key)
    drawn = jax.random.randint(first_key, (RESPONSES,), SPAN_TOKENS // 8, SPAN_TOKENS + 1, dtype=jnp.int32)
    chosen = jax.random.permutation(second_key, RESPONSES)
    drawn = drawn.at[chosen[0]].set(SPAN_TOKENS)
    return drawn.at[chosen[1]].set(SPAN_TOKENS // 8)


def strengthened(values, key, source, target, parts, factor):
    def block_of(dim):
        return (jnp.arange(values.shape[dim]) // (values.shape[dim] // parts)).reshape((-1,) + (1,) * (values.ndim - 1 - dim))

    first = jax.random.permutation(key, parts)[block_of(target)]
    second = (block_of(target) + parts // 2) % parts
    return jnp.where((block_of(source) == first) | (block_of(source) == second), factor * values, values)


def shard_levels(rng, dims, shards, least, high):
    loudness, own = 1.0, jax.random.fold_in(rng, 6)
    for dim, shards_of in shards:
        heights = jnp.exp(jax.random.uniform(jax.random.fold_in(own, dim), (shards_of,), jnp.float32, least / len(shards), high / len(shards)))
        loudness = loudness * jnp.repeat(heights, dims[dim] // shards_of).reshape([-1 if axis == dim else 1 for axis in range(len(dims))])
    return loudness


def centred(own_key, extent, deviation, bound, cuts=(), kind=jnp.bfloat16):
    entries = deviation * jax.random.normal(own_key, extent, jnp.float32)
    if cuts:
        entries = entries * shard_levels(own_key, extent, cuts, -0.22, 0.18)
    return jnp.clip(entries, -bound, bound).astype(kind)


def noise_with(rng, shape, spread, most, pieces, heavy, kind=jnp.bfloat16):
    entries = spread * jax.random.normal(rng, shape, jnp.float32)
    if pieces:
        entries = entries * shard_levels(rng, shape, pieces, -0.22, 0.18)
    return jnp.clip(strengthened(entries, jax.random.fold_in(rng, 3), *heavy), -most, most).astype(kind)


def setup_inputs(seed: int = 0) -> dict:
    arg_keys = jax.random.split(jax.random.key(seed), 9)
    return {
        "normed": noise_with(arg_keys[0], (TOKENS, INPUT_FEATURES), 1.0, 6.0, ((0, 32),), (0, 1, 32, 2.75)),
        "w_query": centred(arg_keys[1], (INPUT_FEATURES, QUERY_HEADS * HEAD_SIZE), INPUT_FEATURES ** -0.5, 0.125, ((1, 4),)),
        "key_weight": centred(arg_keys[2], (INPUT_FEATURES, KEY_HEADS * HEAD_SIZE), INPUT_FEATURES ** -0.5, 0.125, ((1, 4),)),
        "value_weight": centred(arg_keys[3], (INPUT_FEATURES, KEY_HEADS * HEAD_SIZE), INPUT_FEATURES ** -0.5, 0.125, ((1, 4),)),
        "q_gain": jnp.clip(1.0 + 0.15 * jax.random.normal(arg_keys[4], (HEAD_SIZE,), jnp.float32), 0.25, 1.75),
        "key_norm_gain": jnp.clip(1.0 + 0.15 * jax.random.normal(arg_keys[5], (HEAD_SIZE,), jnp.float32), 0.25, 1.75),
        "ctx_grad": centred(arg_keys[6], (TOKENS, QUERY_HEADS * HEAD_SIZE), 1.0, 6.0, ((0, 32),)),
        "lengths": draw_lengths(jax.random.fold_in(arg_keys[8], 71), 0),
    }


epsilon = 1e-06
log_base = math.log(1000000.0)

def angle_tables(length, width):
    position = jnp.arange(length, dtype=jnp.int32).astype(jnp.float32)
    freqs = jnp.exp(jnp.arange(width // 2, dtype=jnp.float32) * (-2.0 * log_base / width))
    angles = position[:, None] * freqs[None, :]
    cosine_table = jnp.cos(angles)
    sine_values = jnp.sin(angles)
    return (jnp.concatenate([cosine_table, cosine_table], 1), jnp.concatenate([sine_values, sine_values], 1))

def turned(values):
    half = values.shape[-1] // 2
    return jnp.concatenate([-values[..., half:], values[..., :half]], -1)

def rotate_pairs(values, cosine_table, sine_values):
    return values * cosine_table + turned(values) * sine_values

def inverse_rotation(grads, cosine_table, sine_values):
    return grads * cosine_table - turned(grads) * sine_values

def normalize(values, gain):
    inverse = lax.rsqrt(lax.optimization_barrier(jnp.mean(values * values, -1, keepdims=True)) + epsilon)
    return (values * inverse * gain, inverse)

def head_norm_gradient(values, inverse, gain, grads):
    weighted = gain * grads
    return inverse * weighted - values * (inverse * inverse * inverse) * lax.optimization_barrier(jnp.mean(values * weighted, -1, keepdims=True))

def reference(normed, w_query, key_weight, value_weight, q_gain, key_norm_gain, ctx_grad, lengths):
    scale_factor = HEAD_SIZE ** (-0.5)
    inputs = normed.reshape(RESPONSES, SPAN_TOKENS, INPUT_FEATURES)
    cotangents = ctx_grad.reshape(RESPONSES, SPAN_TOKENS, QUERY_HEADS * HEAD_SIZE)
    positions = jnp.arange(SPAN_TOKENS, dtype=jnp.int32)
    combined_width = (QUERY_HEADS + 2 * KEY_HEADS) * HEAD_SIZE
    cosine_base, sine_base = angle_tables(SPAN_TOKENS, HEAD_SIZE)
    cosine_table = cosine_base[:, None, :]
    sine_values = sine_base[:, None, :]

    def one_response(running_total, response):
        token_rows, output_cotangent, length = response
        q_proj = jnp.dot(token_rows, w_query, preferred_element_type=jnp.float32).reshape(SPAN_TOKENS, QUERY_HEADS, HEAD_SIZE)
        key_projected = jnp.dot(token_rows, key_weight, preferred_element_type=jnp.float32).reshape(SPAN_TOKENS, KEY_HEADS, HEAD_SIZE)
        value_row_block = jnp.dot(token_rows, value_weight, preferred_element_type=jnp.float32).astype(jnp.bfloat16).reshape(SPAN_TOKENS, KEY_HEADS, HEAD_SIZE)
        q_normed, q_inverse = normalize(q_proj, q_gain)
        k_normed, key_inverse_norm = normalize(key_projected, key_norm_gain)
        query_matrix = rotate_pairs(q_normed, cosine_table, sine_values).astype(jnp.bfloat16)
        key_rows = rotate_pairs(k_normed, cosine_table, sine_values).astype(jnp.bfloat16)
        unmasked_rows = positions < length
        allowed = (positions[None, :] <= positions[:, None]) & unmasked_rows[None, :]
        output_gradient = jnp.where(unmasked_rows[:, None], output_cotangent, jnp.zeros((), jnp.bfloat16)).reshape(SPAN_TOKENS, KEY_HEADS, QUERY_PER_KV, HEAD_SIZE)
        query_full_width = query_matrix.reshape(SPAN_TOKENS, KEY_HEADS, QUERY_PER_KV, HEAD_SIZE).astype(jnp.float32)
        key_wide = key_rows.astype(jnp.float32)
        value_wide = value_row_block.astype(jnp.float32)
        gradient_full_width = output_gradient.astype(jnp.float32)
        scores = jnp.einsum('ikgd,jkd->kgij', query_full_width, key_wide) * scale_factor
        weights = jnp.where(allowed, jnp.exp(scores), jnp.zeros((), jnp.float32))
        probs = weights / lax.optimization_barrier(jnp.sum(weights, -1, keepdims=True))
        probabilities_reduced = lax.optimization_barrier(probs.astype(jnp.bfloat16)).astype(jnp.float32)
        context = jnp.einsum('kgij,jkd->ikgd', probabilities_reduced, value_wide)
        delta = lax.optimization_barrier(jnp.sum(gradient_full_width * context, -1))
        dprob = jnp.einsum('ikgd,jkd->kgij', gradient_full_width, value_wide)
        dscore = probs * (dprob - jnp.transpose(delta, (1, 2, 0))[..., None])
        dscore_low = lax.optimization_barrier(dscore.astype(jnp.bfloat16)).astype(jnp.float32)
        dq_rot = jnp.einsum('kgij,jkd->ikgd', dscore_low, key_wide).reshape(SPAN_TOKENS, QUERY_HEADS, HEAD_SIZE) * scale_factor
        rotated_key_gradient = jnp.einsum('lufr,flux->rlx', dscore_low, query_full_width) * scale_factor
        value_gradient = jnp.einsum('lufr,flux->rlx', probabilities_reduced, gradient_full_width).astype(jnp.bfloat16).reshape(SPAN_TOKENS, KEY_HEADS * HEAD_SIZE)
        query_grad = head_norm_gradient(q_proj, q_inverse, q_gain, inverse_rotation(dq_rot, cosine_table, sine_values)).astype(jnp.bfloat16).reshape(SPAN_TOKENS, QUERY_HEADS * HEAD_SIZE)
        key_gradient = head_norm_gradient(key_projected, key_inverse_norm, key_norm_gain, inverse_rotation(rotated_key_gradient, cosine_table, sine_values)).astype(jnp.bfloat16).reshape(SPAN_TOKENS, KEY_HEADS * HEAD_SIZE)
        input_grad = jnp.dot(query_grad, w_query.T, preferred_element_type=jnp.float32)
        input_grad = input_grad + jnp.dot(key_gradient, key_weight.T, preferred_element_type=jnp.float32)
        input_grad = input_grad + jnp.dot(value_gradient, value_weight.T, preferred_element_type=jnp.float32)
        stacked = jnp.concatenate([query_grad, key_gradient, value_gradient], 1)
        running_total = running_total + jnp.dot(token_rows.T, stacked, preferred_element_type=jnp.float32)
        return (running_total, input_grad.astype(jnp.bfloat16))
    running_total, input_grads = lax.scan(one_response, jnp.zeros((INPUT_FEATURES, combined_width), jnp.float32), (inputs, cotangents, lengths))
    normed_input_gradient = input_grads.reshape(RESPONSES * SPAN_TOKENS, INPUT_FEATURES)
    return (normed_input_gradient, running_total[:, :QUERY_HEADS * HEAD_SIZE], running_total[:, QUERY_HEADS * HEAD_SIZE:(QUERY_HEADS + KEY_HEADS) * HEAD_SIZE], running_total[:, (QUERY_HEADS + KEY_HEADS) * HEAD_SIZE:])
```

```python
import functools
import math

import jax
import jax.numpy as jnp
from jax import lax
from jax.experimental import pallas as pl
from jax.experimental.pallas import tpu as pltpu
from jax.sharding import PartitionSpec as P

epsilon = 1e-06
log_base = math.log(1000000.0)
bf16 = jnp.bfloat16
f32 = jnp.float32
MIB = 1024 * 1024


def cost(flops):
    return pl.CostEstimate(flops=int(flops), bytes_accessed=1024, transcendentals=0)


def waiting(deps, kernel, first=0):
    def body(*refs):
        return kernel(*refs[:first], *refs[first + len(deps) :])

    return body


ANY = pl.BlockSpec(memory_space=pl.ANY)


def angle_tables(length, width):
    position = jnp.arange(length, dtype=jnp.int32).astype(f32)
    freqs = jnp.exp(jnp.arange(width // 2, dtype=f32) * (-2.0 * log_base / width))
    angles = position[:, None] * freqs[None, :]
    cosine = jnp.cos(angles)
    sine = jnp.sin(angles)
    return jnp.concatenate([cosine, cosine], 1), jnp.concatenate([-sine, sine], 1)


def exchange(value, axis, size, bit):
    return lax.ppermute(value, axis, [(d, d ^ bit) for d in range(size)])


def roll_half(a):
    return pltpu.roll(a, a.shape[-1] // 2, a.ndim - 1)


def norm_gradient(values, gain, grads):
    inverse = lax.rsqrt(jnp.mean(values * values, -1, keepdims=True) + epsilon)
    weighted = gain * grads
    mean = jnp.mean(values * weighted, -1, keepdims=True)
    return inverse * weighted - values * (inverse * inverse * inverse * mean)


def projection_kernel(me, s0, s1, wq, wk, wv, q_gain, k_gain, cosine, signed, *rest):
    q_out, u_out, k_out, kp_out, v_out, span = rest[-6:]
    step = pl.program_id(0)
    rows = s0.shape[0]
    width = q_gain.shape[1]

    def normed_rotated(u, gain):
        inverse = lax.rsqrt(jnp.mean(u * u, -1, keepdims=True) + epsilon)
        a = u * inverse * gain
        return (a * cosine[...] + roll_half(a) * signed[...]).astype(bf16)

    @pl.when(step == 0)
    def _():
        for m, s in enumerate((s0, s1)):
            at = pl.multiple_of(((me[0] & 1) ^ m) * rows, rows)
            span[pl.ds(at, rows), :] = s[...]
        both = jnp.concatenate([wk[...], wv[...]], 1)
        kv = jnp.dot(span[...], both, preferred_element_type=f32)
        kp_out[...] = kv[:, :width]
        k_out[...] = normed_rotated(kv[:, :width], k_gain[...])
        v_out[...] = kv[:, width:].astype(bf16)

    @pl.when(step > 0)
    def _():
        u = jnp.dot(span[...], wq[...], preferred_element_type=f32)
        u_out[...] = u
        for h in range(u.shape[1] // width):
            part = slice(h * width, (h + 1) * width)
            q_out[:, part] = normed_rotated(u[:, part], q_gain[...])


def projections(me, flip, pair, wq, wk, wv, q_gain, k_gain, cosine, signed, block, previous):
    rows, features = pair[0].shape
    length = cosine.shape[0]
    half = 2 * rows
    columns, width = wq.shape[1], wk.shape[1]
    steps = columns // block + 1

    def whole(a):
        return pl.BlockSpec(a.shape, lambda i, me: (0, 0))

    def rows_of(me):
        return (me[0] >> 1) ^ flip

    def column_of(i):
        return jnp.maximum(i - 1, 0)

    table = pl.BlockSpec((half, width), lambda i, me: (rows_of(me), 0))
    wide = pl.BlockSpec((half, block), lambda i, me: (rows_of(me), column_of(i)))
    shape = jax.ShapeDtypeStruct
    inputs = (me, *pair, wq, wk, wv, q_gain, k_gain, cosine, signed)
    return pl.pallas_call(
        projection_kernel,
        grid_spec=pltpu.PrefetchScalarGridSpec(
            num_scalar_prefetch=1,
            grid=(steps,),
            in_specs=[whole(s) for s in pair]
            + [pl.BlockSpec((features, block), lambda i, me: (0, column_of(i)))]
            + [whole(a) for a in (wk, wv, q_gain, k_gain)]
            + [table, table]
            + [pl.BlockSpec(memory_space=pl.ANY)] * len(previous),
            out_specs=[wide, wide, table, table, table],
            scratch_shapes=[pltpu.VMEM((half, features), bf16)],
        ),
        out_shape=[
            shape((length, columns), bf16),
            shape((length, columns), f32),
            shape((length, width), bf16),
            shape((length, width), f32),
            shape((length, width), bf16),
        ],
        input_output_aliases={len(inputs) + n: n for n in range(len(previous))},
        compiler_params=pltpu.CompilerParams(vmem_limit_bytes=40 * MIB),
        cost_estimate=cost(2 * half * features * (columns + 2 * width)),
        name="projections",
    )(*inputs, *previous)


def transpose_kernel(me, s0, s1, out):
    rows = s0.shape[0]
    for m, s in enumerate((s0, s1)):
        at = pl.multiple_of(((me[0] & 1) ^ m) * rows, rows)
        out[:, pl.ds(at, rows)] = s[...].T


def transposed(me, pair, deps=()):
    rows, features = pair[0].shape
    block = features
    for size in (256, 128):
        if features % size == 0:
            block = size
            break
    return pl.pallas_call(
        waiting(deps, transpose_kernel),
        grid=(features // block,),
        in_specs=[ANY] * len(deps)
        + [pl.BlockSpec(memory_space=pltpu.SMEM)]
        + [pl.BlockSpec((rows, block), lambda i: (0, i))] * 2,
        out_specs=pl.BlockSpec((block, 2 * rows), lambda i: (i, 0)),
        out_shape=jax.ShapeDtypeStruct((features, 2 * rows), bf16),
        compiler_params=pltpu.CompilerParams(vmem_limit_bytes=32 * MIB),
        cost_estimate=cost(2 * rows * features * 512),
        name="transposed",
    )(*deps, me, *pair)


def attention_kernel(
    tile, me, lengths, q, u, k, v, c0, c1, c2, c3, q_gain, cosine, signed,
    dk_in, dv_in, kp, k_gain, qg_out, dk_out, dv_out, d_out,
):
    length, width = k.shape
    heads = q.shape[1] // width
    rows = c0.shape[0]
    scale = width ** (-0.5)
    constant = scale * math.log2(math.e)
    valid = lengths[0]
    for m, c in enumerate((c0, c1, c2, c3)):
        at = pl.multiple_of((me[0] ^ m) * rows, rows)
        position = lax.broadcasted_iota(jnp.int32, c.shape, 0) + at
        kept = jnp.where(position < valid, c[...].astype(f32), 0.0)
        d_out[pl.ds(at, rows), :] = kept.astype(bf16)
    dk_out[...] = dk_in[...]
    dv_out[...] = dv_in[...]
    for block in range(length // tile):
        here = slice(block * tile, (block + 1) * tile)
        seen = slice(0, (block + 1) * tile)
        keys = lax.broadcasted_iota(jnp.int32, ((block + 1) * tile, tile), 0)
        queries = lax.broadcasted_iota(jnp.int32, ((block + 1) * tile, tile), 1) + block * tile
        allowed = (keys <= queries) & (keys < valid)
        for h in range(heads):
            part = slice(h * width, (h + 1) * width)
            q_head = q[here, part]
            o_grad = d_out[here, part]
            scores = lax.dot_general(
                k[seen, :], q_head, (((1,), (1,)), ((), ())), preferred_element_type=f32
            )
            weights = jnp.where(allowed, jnp.exp2(scores * constant), 0.0)
            probs = weights * (1.0 / jnp.sum(weights, 0, keepdims=True))
            low = probs.astype(bf16)
            dprob = lax.dot_general(
                v[seen, :], o_grad, (((1,), (1,)), ((), ())), preferred_element_type=f32
            )
            delta = jnp.sum(low.astype(f32) * dprob, 0, keepdims=True)
            dscore = (probs * (dprob - delta)).astype(bf16)
            dq = lax.dot_general(
                dscore, k[seen, :], (((0,), (0,)), ((), ())), preferred_element_type=f32
            ) * scale
            dk_out[seen, :] += jnp.dot(dscore, q_head, preferred_element_type=f32)
            dv_out[seen, :] += jnp.dot(low, o_grad, preferred_element_type=f32)
            back = dq * cosine[here, :] - roll_half(dq) * signed[here, :]
            qg_out[here, part] = norm_gradient(u[here, part], q_gain[...], back).astype(bf16)


def attention_last_kernel(tile, *refs):
    *inputs, qg_out, kv_out, d_out, dk_out, dv_out = refs
    attention_kernel(tile, *inputs, qg_out, dk_out, dv_out, d_out)
    cosine, signed, _, _, kp, k_gain = inputs[-6:]
    width = kp.shape[1]
    scale = width ** (-0.5)
    dk = dk_out[...] * scale
    back = dk * cosine[...] - roll_half(dk) * signed[...]
    kv_out[:, :width] = norm_gradient(kp[...], k_gain[...], back).astype(bf16)
    kv_out[:, width:] = dv_out[...].astype(bf16)


def attention(group, last, block, me, lengths, q, u, k, v, cs, q_gain, cosine, signed, dk, dv, kp, k_gain, deps):
    length, width = k.shape
    rows = cs[0].shape[0]
    tile = min(256, length)

    def whole(a):
        return pl.BlockSpec(a.shape, lambda i: (0, 0))

    part = pl.BlockSpec((length, block), lambda i: (0, group))
    out = pl.BlockSpec((length, block), lambda i: (0, 0))
    sums = pl.BlockSpec((length, width), lambda i: (0, 0))
    shape = jax.ShapeDtypeStruct
    if last:
        kernel = functools.partial(attention_last_kernel, tile)
        out_specs = [out, pl.BlockSpec((length, 2 * width), lambda i: (0, 0))]
        out_shape = [shape((length, block), bf16), shape((length, 2 * width), bf16)]
        scratch = [pltpu.VMEM((length, block), bf16)] + [pltpu.VMEM((length, width), f32)] * 2
    else:
        kernel = functools.partial(attention_kernel, tile)
        out_specs = [out, sums, sums]
        out_shape = [shape((length, block), bf16)] + [shape((length, width), f32)] * 2
        scratch = [pltpu.VMEM((length, block), bf16)]
    heads = block // width
    return pl.pallas_call(
        waiting(deps, kernel),
        grid=(1,),
        in_specs=[ANY] * len(deps)
        + [pl.BlockSpec(memory_space=pltpu.SMEM)] * 2
        + [part, part, whole(k), whole(v)]
        + [pl.BlockSpec((rows, block), lambda i: (0, group))] * len(cs)
        + [whole(a) for a in (q_gain, cosine, signed, dk, dv, kp, k_gain)],
        out_specs=out_specs,
        out_shape=out_shape,
        scratch_shapes=scratch,
        compiler_params=pltpu.CompilerParams(vmem_limit_bytes=48 * MIB),
        cost_estimate=cost(1.3e9),
        name="attention",
    )(*deps, me, lengths, q, u, k, v, *cs, q_gain, cosine, signed, dk, dv, kp, k_gain)


def weight_kernel(me, own_a, own_b, other_a, other_b, own_g, other_g, send, keep):
    step = pl.program_id(0)
    half = own_a.shape[1]
    first = pl.multiple_of((me[0] >> 1) * half, half)
    second = pl.multiple_of(((me[0] >> 1) ^ 1) * half, half)

    lhs = jnp.concatenate([own_a[...], own_b[...], other_a[...], other_b[...]], 1)
    rhs = [g[pl.ds(at, half), :] for g in (own_g, other_g) for at in (first, second)]
    total = jnp.dot(lhs, jnp.concatenate(rhs, 0), preferred_element_type=f32)

    @pl.when(step == 0)
    def _():
        send[...] = total.astype(bf16)

    @pl.when(step == 1)
    def _():
        keep[...] = total


def weight_products(me, transposes, own_g, other_g, deps, last):
    features, half = transposes[0].shape
    length, columns = own_g.shape
    out = pl.BlockSpec((features // 2, columns), lambda i: (0, 0))
    return pl.pallas_call(
        waiting(deps, weight_kernel),
        grid=(2,),
        in_specs=[ANY] * len(deps)
        + [pl.BlockSpec(memory_space=pltpu.SMEM)]
        + [pl.BlockSpec((features // 2, half), lambda i: (i, 0))] * 4
        + [pl.BlockSpec((length, columns), lambda i: (0, 0))] * 2,
        out_specs=[out, out],
        out_shape=[
            jax.ShapeDtypeStruct((features // 2, columns), bf16),
            jax.ShapeDtypeStruct((features // 2, columns), f32),
        ],
        compiler_params=pltpu.CompilerParams(vmem_limit_bytes=32 * MIB),
        cost_estimate=cost(3e10 if last else 1.2e9),
        name="weight_products",
    )(*deps, me, *transposes, own_g, other_g)


def input_kernel(me, *refs):
    *parts, kv, wq, wk, wv, send, keep, grads = refs
    half = send.shape[0]
    rows = half // 2
    block = parts[0].shape[1]

    @pl.when(pl.program_id(0) == 0)
    def _():
        for other in range(2):
            for chip in range(2):
                at = pl.multiple_of((2 * chip + (1 - other) * (1 - me[0]) + other * me[0]) * rows, rows)
                here = slice((2 * other + chip) * rows, (2 * other + chip + 1) * rows)
                for g, ref in enumerate((*parts, kv)):
                    grads[here, g * block : (g + 1) * block] = ref[pl.ds(at, rows), :]

    weights = jnp.concatenate([wq[...], wk[...], wv[...]], 1)
    total = lax.dot_general(
        grads[...], weights, (((1,), (1,)), ((), ())), preferred_element_type=f32
    )
    send[...] = total[:half].astype(bf16)
    keep[...] = total[half:]


def input_products(core, parts, kv, wq, wk, wv, deps):
    length = kv.shape[0]
    features, columns = wq.shape
    width = wk.shape[1]
    tile = 512 if features % 512 == 0 else features
    out = pl.BlockSpec((length // 2, tile), lambda i: (0, i))
    return pl.pallas_call(
        waiting(deps, input_kernel),
        grid=(features // tile,),
        in_specs=[ANY] * len(deps)
        + [pl.BlockSpec(memory_space=pltpu.SMEM)]
        + [pl.BlockSpec(a.shape, lambda i: (0, 0)) for a in (*parts, kv)]
        + [pl.BlockSpec((tile, a.shape[1]), lambda i: (i, 0)) for a in (wq, wk, wv)],
        out_specs=[out, out],
        out_shape=[
            jax.ShapeDtypeStruct((length // 2, features), bf16),
            jax.ShapeDtypeStruct((length // 2, features), f32),
        ],
        scratch_shapes=[pltpu.VMEM((length, columns + 2 * width), bf16)],
        compiler_params=pltpu.CompilerParams(vmem_limit_bytes=32 * MIB),
        cost_estimate=cost(1e6),
        name="input_products",
    )(*deps, core.astype(jnp.int32).reshape(1), *parts, kv, wq, wk, wv)


def final_kernel(*refs):
    *inputs, query_out, key_out, value_out = refs
    width = key_out.shape[1]
    count = len(inputs) // 2
    for n in range(count):
        total = inputs[n][...] + inputs[count + n][...].astype(f32)
        columns = total.shape[1]
        if n < count - 1:
            query_out[:, n * columns : (n + 1) * columns] = total
        else:
            key_out[...] = total[:, :width]
            value_out[...] = total[:, width:]


def final_sums(ends, width):
    share, columns = ends[0][1].shape
    kept = [end[0] for end in ends]
    received = [end[1] for end in ends]

    def spec(columns, block=0):
        return pl.BlockSpec((share, columns), lambda i: (block, 0))

    widths = ((len(ends) - 1) * columns, width, width)
    return pl.pallas_call(
        final_kernel,
        grid=(1,),
        in_specs=[spec(columns, 1)] * len(ends) + [spec(columns)] * len(ends),
        out_specs=[spec(w) for w in widths],
        out_shape=[jax.ShapeDtypeStruct((share, w), f32) for w in widths],
        compiler_params=pltpu.CompilerParams(vmem_limit_bytes=32 * MIB),
        cost_estimate=cost(1024),
        name="final_sums",
    )(*kept, *received)


def local(dp, sp, normed, wq, wk, wv, q_gain, k_gain, ctx_grad, lengths):
    rows, features = normed.shape
    width = q_gain.shape[0]
    columns = wq.shape[1]
    length = rows * sp
    block = 2 * width
    me_sp = lax.axis_index("sp")
    me_dp = lax.axis_index("dp")
    core, chip = me_sp % 2, me_sp // 2
    me = me_sp.astype(jnp.int32).reshape(1)
    q_gain = q_gain.reshape(1, width)
    k_gain = k_gain.reshape(1, width)
    cosine, signed = angle_tables(length, width)
    over_sp = functools.partial(exchange, axis="sp", size=sp)
    over_dp = functools.partial(exchange, axis="dp", size=dp)
    pair_bit = 2 if dp > 2 else 1
    halving = [b for b in (1 << i for i in range(dp.bit_length() - 1)) if b != pair_bit]
    share = features // dp
    mine = (me_dp // pair_bit) % 2

    def theirs(rows_of):
        size = pair_bit * share
        return jnp.concatenate(
            [
                lax.dynamic_slice_in_dim(rows_of, (2 * i + 1 - mine) * size, size, 1)
                for i in range(features // (2 * size))
            ],
            1,
        )

    def cotangent(m):
        return lax.dynamic_slice_in_dim(ctx_grad, (me_sp ^ m) * columns, columns, 1)

    far = over_sp(normed, bit=2)
    near = over_sp(normed, bit=1)
    pair0 = over_dp(theirs(normed), bit=pair_bit)

    previous = projections(
        me, 0, (normed, near), wq, wk, wv, q_gain, k_gain, cosine, signed, block, ()
    )
    own_a = transposed(me, (normed, near))
    cots = [cotangent(m) for m in range(4)]
    far, pair0, own_a, *rest = lax.optimization_barrier((far, pair0, own_a, *previous, *cots))
    previous, cots = rest[: len(previous)], rest[len(previous) :]

    diagonal = over_sp(far, bit=1)
    cs = (cots[0],) + tuple(over_sp(cots[m], bit=m) for m in (1, 2, 3))
    pair2 = over_dp(theirs(far), bit=pair_bit)
    q, u, k, kp, v = projections(
        me, 1, (far, diagonal), wq, wk, wv, q_gain, k_gain, cosine, signed, block, previous
    )
    own_b = transposed(me, (far, diagonal), (k,))
    pair0, k = lax.optimization_barrier((pair0, k))
    pair1 = over_sp(pair0, bit=1)

    def wanted(i):
        target = me_dp & pair_bit
        for n, bit in enumerate(halving):
            same = (i >> (len(halving) - 1 - n)) & 1
            target = target | ((me_dp if same else ~me_dp) & bit)
        return target

    def compact(d):
        return (d // (2 * pair_bit)) * pair_bit + d % pair_bit

    def ordered(t, place):
        t = t.reshape(t.shape[0] // share, share, t.shape[1])
        return jnp.concatenate(
            [lax.dynamic_index_in_dim(t, place(wanted(i)), 0, False) for i in range(dp // 2)], 0
        )

    own_a = ordered(own_a, lambda d: d)
    own_b = ordered(own_b, lambda d: d)

    groups = columns // block
    dk = jnp.zeros((length, width), f32)
    dv = dk
    parts, received, firsts = [], [], []

    def heads(g, deps):
        result = attention(
            g, g == groups - 1, block, me, lengths, q, u, k, v, cs,
            q_gain, cosine, signed, dk, dv, kp, k_gain, deps,
        )
        parts.append(result[0])
        received.append(over_dp(result[0], bit=pair_bit))
        return result[1:]

    def product(n, deps):
        send, keep = weight_products(
            me, (own_a, own_b, other_a, other_b), parts[n], received[n], deps, n == groups
        )
        firsts.append(keep + over_dp(send, bit=halving[0]).astype(f32))
        return keep

    def last_steps(keep):
        for bit in halving[1:-1]:
            half = keep.shape[0] // 2
            send, keep = keep[:half].astype(bf16), keep[half:]
            keep = keep + over_dp(send, bit=bit).astype(f32)
        return keep, over_dp(keep[:share].astype(bf16), bit=halving[-1])

    dk, dv = heads(0, (own_b,))
    other_a = transposed(me, (pair0, pair1), (dk,))
    pair2, dk = lax.optimization_barrier((pair2, dk))
    pair3 = over_sp(pair2, bit=1)
    dk, dv = heads(1, (other_a,))
    other_b = transposed(me, (pair2, pair3), (dk,))
    dk, dv = heads(2, (other_b,))
    other_a, other_b = ordered(other_a, compact), ordered(other_b, compact)
    keep = product(0, (dk,))
    (kv,) = heads(3, (keep, received[1]))
    parts.append(kv)
    received.append(over_dp(kv, bit=pair_bit))
    keep = product(1, (kv,))
    keep = product(2, (keep, firsts[0]))
    keep = product(3, (keep, firsts[1]))
    sent, kept = input_products(core, parts[:-1], kv, wq, wk, wv, (keep,))
    sent_near = over_sp(sent, bit=1)
    ends = [last_steps(first) for first in firsts]
    product(4, (sent, firsts[2], ends[0][1]))
    kept = (kept + sent_near.astype(f32)).reshape(sp // 2, rows, features)
    sent = lax.dynamic_index_in_dim(kept, 1 - chip, 0, False).astype(bf16)
    sent_far = over_sp(sent, bit=2)
    ends.append(last_steps(firsts[4]))
    kept = lax.dynamic_index_in_dim(kept, chip, 0, False)
    input_gradient = (kept + sent_far.astype(f32)).astype(bf16)
    return (input_gradient, *final_sums(ends, width))


def solution(mesh):
    in_specs = (
        P(("dp", "sp"), None),
        P(None, "sp"),
        P(None, "sp"),
        P(None, "sp"),
        P(),
        P(),
        P(("dp", "sp"), None),
        P("dp"),
    )
    out_specs = (P(("dp", "sp"), None), P("dp", "sp"), P("dp", "sp"), P("dp", "sp"))
    body = functools.partial(local, mesh.shape["dp"], mesh.shape["sp"])
    return jax.shard_map(body, mesh=mesh, in_specs=in_specs, out_specs=out_specs, check_vma=False)
```

```python
import functools
import math

import jax
import jax.numpy as jnp
from jax import lax
from jax.experimental import pallas as pl
from jax.experimental.pallas import tpu as pltpu
from jax.sharding import PartitionSpec as P

epsilon = 1e-06
log_base = math.log(1000000.0)
bf16 = jnp.bfloat16
f32 = jnp.float32
MIB = 1024 * 1024
LONG = 2.3e10
SHORT = 1e6
SMEM = pl.BlockSpec(memory_space=pltpu.SMEM)
VMEM = pl.BlockSpec(memory_space=pltpu.VMEM)
ANY = pl.BlockSpec(memory_space=pl.ANY)


def call(kernel, scalars, inputs, outputs, name, flops, deps=(), scratch=(), aliases=None, limit=14):
    count = len(deps)

    def body(*refs):
        return kernel(*refs[count:])

    return pl.pallas_call(
        body,
        in_specs=[ANY] * count + [SMEM] * len(scalars) + [VMEM] * len(inputs),
        out_specs=[VMEM] * len(outputs),
        out_shape=[jax.ShapeDtypeStruct(shape, dtype) for shape, dtype in outputs],
        scratch_shapes=list(scratch),
        input_output_aliases={
            count + len(scalars) + i: o for i, o in (aliases or {}).items()
        },
        compiler_params=pltpu.CompilerParams(vmem_limit_bytes=limit * MIB),
        cost_estimate=pl.CostEstimate(
            flops=int(flops), bytes_accessed=1024, transcendentals=0
        ),
        name=name,
    )(*deps, *scalars, *inputs)


def angle_tables(length, width):
    position = jnp.arange(length, dtype=jnp.int32).astype(f32)
    freqs = jnp.exp(jnp.arange(width // 2, dtype=f32) * (-2.0 * log_base / width))
    angles = position[:, None] * freqs[None, :]
    cosine = jnp.cos(angles)
    sine = jnp.sin(angles)
    return jnp.concatenate([cosine, cosine], 1), jnp.concatenate([-sine, sine], 1)


def exchange(value, axis, size, bit):
    return lax.ppermute(value, axis, [(d, d ^ bit) for d in range(size)])


def roll_half(a):
    return pltpu.roll(a, a.shape[-1] // 2, a.ndim - 1)


def norm_gradient(values, gain, grads):
    inverse = lax.rsqrt(jnp.mean(values * values, -1, keepdims=True) + epsilon)
    weighted = gain * grads
    mean = jnp.mean(values * weighted, -1, keepdims=True)
    return inverse * weighted - values * (inverse * inverse * inverse * mean)


def place(me, m, rows):
    return pl.ds(pl.multiple_of((me[0] ^ m) * rows, rows), rows)


def projection_kernel(marks, block, me, s0, s1, wq, wk, wv, q_gain, k_gain, cosine, signed, *rest):
    q_out, u_out, k_out, kp_out, v_out = rest[-5:]
    rows = s0.shape[0]
    width = wk.shape[1]
    span = jnp.concatenate([s0[...], s1[...]], 0)

    def normed_rotated(u, gain, at):
        inverse = lax.rsqrt(jnp.mean(u * u, -1, keepdims=True) + epsilon)
        a = u * inverse * gain[...]
        return (a * cosine[at, :] + roll_half(a) * signed[at, :]).astype(bf16)

    kv = jnp.dot(span, jnp.concatenate([wk[...], wv[...]], 1), preferred_element_type=f32)
    for n, m in enumerate(marks):
        at = place(me, m, rows)
        here = kv[n * rows : (n + 1) * rows]
        kp_out[at, :] = here[:, :width]
        k_out[at, :] = normed_rotated(here[:, :width], k_gain, at)
        v_out[at, :] = here[:, width:].astype(bf16)

    @pl.loop(0, wq.shape[1] // block)
    def _(step):
        start = pl.multiple_of(step * block, block)
        span = jnp.concatenate([s0[...], s1[...]], 0)
        u = jnp.dot(span, wq[:, pl.ds(start, block)], preferred_element_type=f32)
        for n, m in enumerate(marks):
            at = place(me, m, rows)
            for h in range(block // width):
                part = u[n * rows : (n + 1) * rows, h * width : (h + 1) * width]
                columns = pl.ds(pl.multiple_of(start + h * width, width), width)
                u_out[at, columns] = part
                q_out[at, columns] = normed_rotated(part, q_gain, at)


def projections(me, marks, pair, wq, wk, wv, q_gain, k_gain, cosine, signed, previous):
    rows = pair[0].shape[0]
    length = cosine.shape[0]
    columns, width = wq.shape[1], wk.shape[1]
    inputs = (*pair, wq, wk, wv, q_gain, k_gain, cosine, signed)
    return call(
        functools.partial(projection_kernel, marks, 2 * width),
        (me,),
        (*inputs, *previous),
        [
            ((length, columns), bf16),
            ((length, columns), f32),
            ((length, width), bf16),
            ((length, width), f32),
            ((length, width), bf16),
        ],
        "projections",
        LONG,
        aliases={len(inputs) + n: n for n in range(len(previous))},
    )


class Order:
    def __init__(self, dp, features):
        self.dp = dp
        self.pair = 2 if dp > 2 else 1
        self.halving = [1 << i for i in range(dp.bit_length() - 1) if 1 << i != self.pair]
        self.share = features // dp
        self.group = self.pair * self.share
        self.groups = features // (2 * self.group)
        self.aligned = self.group % 128 == 0 and self.share % 16 == 0

    def rank(self, me, shard):
        result = 0
        for n, bit in enumerate(self.halving):
            same = 1 - (((me ^ shard) // bit) & 1)
            result = result + (same << (len(self.halving) - 1 - n))
        return result

    def wanted(self, me, place):
        target = me & self.pair
        for n, bit in enumerate(self.halving):
            same = (place >> (len(self.halving) - 1 - n)) & 1
            target = target | ((me if same else ~me) & bit)
        return target


def transpose_kernel(order, both, me_dp, *refs):
    count = len(refs) - (2 if both else 1)
    for target in range(2 if both else 1):
        owner = me_dp[0] ^ (order.pair * target)
        side = (owner // order.pair) & 1
        out = refs[count + target]
        for n, source in enumerate(refs[:count]):
            rows = source.shape[0]
            for g in range(order.groups):
                start = pl.multiple_of((2 * g + side) * order.group, order.group)
                turned = source[:, pl.ds(start, order.group)].T
                for low in range(order.pair):
                    shard = (2 * g + side) * order.pair + low
                    at = pl.multiple_of(order.rank(owner, shard) * order.share, order.share)
                    out[pl.ds(at, order.share), n * rows : (n + 1) * rows] = turned[
                        low * order.share : (low + 1) * order.share
                    ]


def transposed(order, me_dp, shards, both, deps=()):
    rows, features = shards[0].shape
    size = (features // 2, rows * len(shards))
    if order.aligned:
        return call(
            functools.partial(transpose_kernel, order, both),
            (me_dp.astype(jnp.int32).reshape(1),),
            shards,
            [(size, bf16)] * (2 if both else 1),
            "transposed",
            1e8,
            deps,
        )
    whole = jnp.concatenate(shards, 0).T.reshape(order.dp, order.share, size[1])
    results = []
    for target in range(2 if both else 1):
        owner = me_dp ^ (order.pair * target)
        results.append(
            jnp.concatenate(
                [
                    lax.dynamic_index_in_dim(whole, order.wanted(owner, i), 0, False)
                    for i in range(order.dp // 2)
                ],
                0,
            )
        )
    return results


def attention_kernel(
    group, block, tile, me, lengths, q, u, k, v, c0, c1, c2, c3, q_gain, cosine, signed, *rest
):
    *sums_in, qg_out, dk_out, dv_out, d_out = rest
    length, width = k.shape
    rows = c0.shape[0]
    base = group * block
    c_base = base % c0.shape[1]
    scale = width ** (-0.5)
    constant = scale * math.log2(math.e)
    valid = lengths[0]
    for m, c in enumerate((c0, c1, c2, c3)):
        at = place(me, m, rows)
        part = c[:, c_base : c_base + block].astype(f32)
        position = lax.broadcasted_iota(jnp.int32, part.shape, 0) + (me[0] ^ m) * rows
        d_out[at, :] = jnp.where(position < valid, part, 0.0).astype(bf16)
    for block_index in range(length // tile):
        here = slice(block_index * tile, (block_index + 1) * tile)
        size = (block_index + 1) * tile
        seen = slice(0, size)
        keys = lax.broadcasted_iota(jnp.int32, (size, tile), 0)
        queries = lax.broadcasted_iota(jnp.int32, (size, tile), 1) + block_index * tile
        allowed = (keys <= queries) & (keys < valid)
        dk_sum = dv_sum = None
        for h in range(block // width):
            part = slice(base + h * width, base + (h + 1) * width)
            local_part = slice(h * width, (h + 1) * width)
            q_head = q[here, part]
            o_grad = d_out[here, local_part]
            scores = lax.dot_general(
                k[seen, :], q_head, (((1,), (1,)), ((), ())), preferred_element_type=f32
            )
            weights = jnp.where(allowed, jnp.exp2(scores * constant), 0.0)
            probs = weights * (1.0 / jnp.sum(weights, 0, keepdims=True))
            low = probs.astype(bf16)
            dprob = lax.dot_general(
                v[seen, :], o_grad, (((1,), (1,)), ((), ())), preferred_element_type=f32
            )
            delta = jnp.sum(low.astype(f32) * dprob, 0, keepdims=True)
            dscore = (probs * (dprob - delta)).astype(bf16)
            dq = lax.dot_general(
                dscore, k[seen, :], (((0,), (0,)), ((), ())), preferred_element_type=f32
            ) * scale
            dk_head = jnp.dot(dscore, q_head, preferred_element_type=f32)
            dv_head = jnp.dot(low, o_grad, preferred_element_type=f32)
            dk_sum = dk_head if dk_sum is None else dk_sum + dk_head
            dv_sum = dv_head if dv_sum is None else dv_sum + dv_head
            back = dq * cosine[here, :] - roll_half(dq) * signed[here, :]
            qg_out[here, local_part] = norm_gradient(u[here, part], q_gain[...], back).astype(bf16)
        for out, total, index in ((dk_out, dk_sum, 0), (dv_out, dv_sum, 1)):
            old = size - tile
            if block_index:
                out[:old, :] += total[:old]
            out[old:size, :] = total[old:]
            if sums_in:
                out[old:size, :] += sums_in[index][old:size, :]


def attention_last_kernel(group, block, tile, *refs):
    *inputs, kp, k_gain, dk_in, dv_in, out, d_out, dk_out, dv_out = refs
    attention_kernel(group, block, tile, *inputs, dk_in, dv_in, out, dk_out, dv_out, d_out)
    cosine, signed = inputs[-2:]
    width = kp.shape[1]
    dk = dk_out[...] * width ** (-0.5)
    back = dk * cosine[...] - roll_half(dk) * signed[...]
    out[:, block : block + width] = norm_gradient(kp[...], k_gain[...], back).astype(bf16)
    out[:, block + width :] = dv_out[...].astype(bf16)


def attention(group, last, block, scalars, inputs, k_inputs, sums, deps, flops):
    length, width = inputs[2].shape
    tile = min(256, length)
    settings = (group, block, tile)
    scratch = [pltpu.VMEM((length, block), bf16)]
    grads = ((length, block), bf16)
    if last:
        return call(
            functools.partial(attention_last_kernel, *settings),
            scalars,
            (*inputs, *k_inputs, *sums),
            [((length, block + 2 * width), bf16)],
            "attention",
            flops,
            deps,
            scratch + [pltpu.VMEM((length, width), f32)] * 2,
        )
    return call(
        functools.partial(attention_kernel, *settings),
        scalars,
        (*inputs, *sums),
        [grads] + [((length, width), f32)] * 2,
        "attention",
        flops,
        deps,
        scratch,
    )


def weight_sums(start, me, transposes, own_g, other_g, send, keep):
    columns = slice(start, start + send.shape[1])
    rows = own_g.shape[0] // 4
    half = send.shape[0]
    rhs = [g[place(me, m, rows), columns] for g in (own_g, other_g) for m in range(4)]
    rhs = jnp.concatenate(rhs, 0)
    for out, at in ((send, 0), (keep, half)):
        lhs = jnp.concatenate([t[at : at + half, :] for t in transposes], 1)
        out[...] = jnp.dot(lhs, rhs, preferred_element_type=f32).astype(out.dtype)


def weight_kernel(start, me, *refs):
    *transposes, own_g, other_g, send, keep = refs
    weight_sums(start, me, transposes, own_g, other_g, send, keep)


def both_kernel(start, count, first, tile, me, *refs):
    transposes, refs = refs[:count], refs[count:]
    own_g, other_g, *parts, wq, wk, wv, send, keep, in_send, in_keep, grads = refs
    weight_sums(start, me, transposes, own_g, other_g, send, keep)
    half = in_send.shape[0]
    rows = half // 2
    block = parts[0].shape[1]
    for n, m in enumerate((3, 1, 2, 0)):
        at = place(me, m, rows)
        for g, ref in enumerate(parts):
            here = slice(g * block, g * block + ref.shape[1])
            grads[n * rows : (n + 1) * rows, here] = ref[at, :]

    @pl.loop(0, in_send.shape[1] // tile)
    def _(step):
        at = pl.ds(pl.multiple_of(first + step * tile, tile), tile)
        to = pl.ds(pl.multiple_of(step * tile, tile), tile)
        weights = jnp.concatenate([wq[at, :], wk[at, :], wv[at, :]], 1)
        total = lax.dot_general(
            grads[...], weights, (((1,), (1,)), ((), ())), preferred_element_type=f32
        )
        in_send[:, to] = total[:half].astype(bf16)
        in_keep[:, to] = total[half:]


def weight_products(me, transposes, start, columns, own_g, other_g, deps, flops, extra=None):
    half = transposes[0].shape[0] // 2
    length = own_g.shape[0]
    outputs = [((half, columns), bf16), ((half, columns), f32)]
    inputs = (*transposes, own_g, other_g)
    if extra is None:
        kernel = functools.partial(weight_kernel, start)
        return call(kernel, (me,), inputs, outputs, "weight_products", flops, deps)
    (first, count), parts, weights = extra
    tile = 256 if count % 256 == 0 else count
    return call(
        functools.partial(both_kernel, start, len(transposes), first, tile),
        (me,),
        (*inputs, *parts, *weights),
        outputs + [((length // 2, count), bf16), ((length // 2, count), f32)],
        "both_products",
        flops,
        deps,
        [pltpu.VMEM((length, sum(p.shape[1] for p in parts)), bf16)],
        limit=16,
    )


def halve_kernel(keep, received, send, rest):
    half = send.shape[0]
    send[...] = (keep[:half] + received[:half].astype(f32)).astype(bf16)
    rest[...] = keep[half:] + received[half:].astype(f32)


def halve(keep, received, deps=()):
    rows, columns = keep.shape
    half = rows // 2
    if half % 16:
        total = keep + received.astype(f32)
        return total[:half].astype(bf16), total[half:]
    size = (half, columns)
    return call(halve_kernel, (), (keep, received), [(size, bf16), (size, f32)], "halve", 1e6, deps)


def input_sum_kernel(*refs):
    *inputs, out = refs
    count = len(inputs) // 2
    columns = inputs[0].shape[1]
    for n in range(count):
        total = inputs[n][...] + inputs[count + n][...].astype(f32)
        out[:, n * columns : (n + 1) * columns] = total.astype(bf16)


def final_kernel(first, *refs):
    *inputs, query_out, key_out, value_out = refs[first:]
    width = key_out.shape[1]
    count = len(inputs) // 2
    for n in range(count):
        total = inputs[n][...] + inputs[count + n][...].astype(f32)
        columns = total.shape[1]
        if n < count - 1:
            query_out[:, n * columns : (n + 1) * columns] = total
        else:
            key_out[...] = total[:, :width]
            value_out[...] = total[:, width:]


def final_sums(ends, width, deps):
    share, columns = ends[0][0].shape
    kept = [end[0] for end in ends]
    received = [end[1] for end in ends]
    widths = ((len(ends) - 1) * columns, width, width)
    return pl.pallas_call(
        functools.partial(final_kernel, len(deps)),
        in_specs=[ANY] * len(deps) + [VMEM] * (2 * len(ends)),
        out_shape=[jax.ShapeDtypeStruct((share, w), f32) for w in widths],
        compiler_params=pltpu.CompilerParams(vmem_limit_bytes=14 * MIB),
        cost_estimate=pl.CostEstimate(flops=1024, bytes_accessed=1024, transcendentals=0),
        name="final_sums",
    )(*deps, *kept, *received)


def local(dp, sp, normed, wq, wk, wv, q_gain, k_gain, ctx_grad, lengths):
    rows, features = normed.shape
    width = q_gain.shape[0]
    columns = wq.shape[1]
    length = rows * sp
    block = 2 * width
    groups = columns // block
    me_sp = lax.axis_index("sp")
    me_dp = lax.axis_index("dp")
    me = me_sp.astype(jnp.int32).reshape(1)
    q_gain = q_gain.reshape(1, width)
    k_gain = k_gain.reshape(1, width)
    cosine, signed = angle_tables(length, width)
    over_sp = functools.partial(exchange, axis="sp", size=sp)
    over_dp = functools.partial(exchange, axis="dp", size=dp)
    order = Order(dp, features)

    def cotangent(m, part):
        size = columns // 2
        return lax.dynamic_slice_in_dim(ctx_grad, (me_sp ^ m) * columns + part * size, size, 1)

    far = over_sp(normed, bit=2)
    near = over_sp(normed, bit=1)

    own_o, pair_o = transposed(order, me_dp, (normed,), True)
    other_o = over_dp(pair_o, bit=order.pair)
    (own_n,) = transposed(order, me_dp, (near,), False)
    previous = projections(
        me, (0, 1), (normed, near), wq, wk, wv, q_gain, k_gain, cosine, signed, ()
    )
    cots = [cotangent(m, part) for part in range(2) for m in range(4)]
    far, other_o, own_n, *rest = lax.optimization_barrier((far, other_o, own_n, *previous, *cots))
    previous, cots = rest[: len(previous)], rest[len(previous) :]

    diagonal = over_sp(far, bit=1)
    cs = [
        (cots[4 * part],) + tuple(over_sp(cots[4 * part + m], bit=m) for m in (1, 2, 3))
        for part in range(2)
    ]
    own_f, pair_f = transposed(order, me_dp, (far,), True)
    other_f = over_dp(pair_f, bit=order.pair)
    q, u, k, kp, v = projections(
        me, (2, 3), (far, diagonal), wq, wk, wv, q_gain, k_gain, cosine, signed, previous
    )
    (own_d,) = transposed(order, me_dp, (diagonal,), False, (k, *cs[0][2:]))

    parts, received, firsts = [], [], []
    sums = ()

    def heads(g, deps, flops):
        inputs = (q, u, k, v, *cs[2 * g // groups], q_gain, cosine, signed)
        result = attention(
            g, g == groups - 1, block, (me, lengths), inputs, (kp, k_gain), sums, deps, flops
        )
        parts.append(result[0])
        received.append(over_dp(result[0], bit=order.pair))
        return result[1:]

    def product(n, deps, flops, extra=None):
        send, keep, *more = weight_products(
            me, (own_o, own_n, own_f, own_d, other_o, other_n, other_f, other_d), max(n - groups + 1, 0) * block, block,
            parts[min(n, groups - 1)], received[min(n, groups - 1)], deps, flops, extra,
        )
        firsts.append((keep, over_dp(send, bit=order.halving[0])))
        return (keep, *more)

    def input_part(n):
        return ((n * features // 2, features // 2), parts, (wq, wk, wv))

    def halved(sent, kept):
        sent, kept = halve(kept, over_sp(sent, bit=1))
        return kept, over_sp(sent, bit=2)

    def last_steps(keep, came, deps=()):
        for bit in order.halving[1:]:
            send, keep = halve(keep, came, deps)
            came = over_dp(send, bit=bit)
        return keep, came

    sums = heads(0, (own_d,), SHORT)
    other_o, other_f, tied = lax.optimization_barrier((other_o, other_f, sums[0]))
    sums = (tied, sums[1])
    other_n, other_d = over_sp(other_o, bit=1), over_sp(other_f, bit=1)
    sums = heads(1, (), LONG)
    sums = heads(2, (received[0],), LONG)
    keep, = product(0, (sums[0],), SHORT)
    heads(3, (keep, received[1]), LONG)
    keep, = product(1, (parts[3],), SHORT)
    ends = [last_steps(*firsts[0])]
    keep, sent, kept = product(2, (keep, ends[0][0]), LONG, input_part(0))
    inputs = [halved(sent, kept)]
    ends.append(last_steps(*firsts[1]))
    keep, sent, kept = product(3, (keep, ends[1][0], ends[0][1]), LONG, input_part(1))
    ends.append(last_steps(*firsts[2]))
    product(4, (keep, ends[2][0], ends[1][1], inputs[0][0]), LONG)
    inputs.append(halved(sent, kept))
    ends.append(last_steps(*firsts[3]))
    ends.append(last_steps(*firsts[4], (ends[2][1],)))
    pieces = [i[0] for i in inputs] + [i[1] for i in inputs]
    input_gradient = pl.pallas_call(
        input_sum_kernel,
        in_specs=[VMEM] * len(pieces),
        out_shape=jax.ShapeDtypeStruct((rows, features), bf16),
        compiler_params=pltpu.CompilerParams(vmem_limit_bytes=14 * MIB),
        cost_estimate=pl.CostEstimate(flops=1024, bytes_accessed=1024, transcendentals=0),
        name="input_sum",
    )(*pieces)
    return (input_gradient, *final_sums(ends, width, (input_gradient,)))


def solution(mesh):
    in_specs = (
        P(("dp", "sp"), None),
        P(None, "sp"),
        P(None, "sp"),
        P(None, "sp"),
        P(),
        P(),
        P(("dp", "sp"), None),
        P("dp"),
    )
    out_specs = (P(("dp", "sp"), None), P("dp", "sp"), P("dp", "sp"), P("dp", "sp"))
    body = functools.partial(local, mesh.shape["dp"], mesh.shape["sp"])
    return jax.shard_map(body, mesh=mesh, in_specs=in_specs, out_specs=out_specs, check_vma=False)
```

```python
import functools
import math

import jax
import jax.numpy as jnp
from jax import lax
from jax.experimental import pallas as pl
from jax.experimental.pallas import tpu as pltpu
from jax.sharding import PartitionSpec as P

epsilon = 1e-06
log_base = math.log(1000000.0)
bf16 = jnp.bfloat16
f32 = jnp.float32
MIB = 1024 * 1024
LONG = 2.3e10
SHORT = 1e6
SMEM = pl.BlockSpec(memory_space=pltpu.SMEM)
VMEM = pl.BlockSpec(memory_space=pltpu.VMEM)
ANY = pl.BlockSpec(memory_space=pl.ANY)


def call(kernel, scalars, inputs, outputs, name, flops, deps=(), scratch=(), aliases=None, limit=14):
    count = len(deps)

    def body(*refs):
        return kernel(*refs[count:])

    return pl.pallas_call(
        body,
        in_specs=[ANY] * count + [SMEM] * len(scalars) + [VMEM] * len(inputs),
        out_specs=[VMEM] * len(outputs),
        out_shape=[jax.ShapeDtypeStruct(shape, dtype) for shape, dtype in outputs],
        scratch_shapes=list(scratch),
        input_output_aliases={
            count + len(scalars) + i: o for i, o in (aliases or {}).items()
        },
        compiler_params=pltpu.CompilerParams(vmem_limit_bytes=limit * MIB),
        cost_estimate=pl.CostEstimate(
            flops=int(flops), bytes_accessed=1024, transcendentals=0
        ),
        name=name,
    )(*deps, *scalars, *inputs)


def angle_tables(length, width):
    position = jnp.arange(length, dtype=jnp.int32).astype(f32)
    freqs = jnp.exp(jnp.arange(width // 2, dtype=f32) * (-2.0 * log_base / width))
    angles = position[:, None] * freqs[None, :]
    cosine = jnp.cos(angles)
    sine = jnp.sin(angles)
    return jnp.concatenate([cosine, cosine], 1), jnp.concatenate([-sine, sine], 1)


def exchange(value, axis, size, bit):
    return lax.ppermute(value, axis, [(d, d ^ bit) for d in range(size)])


def roll_half(a):
    return pltpu.roll(a, a.shape[-1] // 2, a.ndim - 1)


def norm_gradient(values, gain, grads):
    inverse = lax.rsqrt(jnp.mean(values * values, -1, keepdims=True) + epsilon)
    weighted = gain * grads
    mean = jnp.mean(values * weighted, -1, keepdims=True)
    return inverse * weighted - values * (inverse * inverse * inverse * mean)


def place(me, m, rows):
    return pl.ds(pl.multiple_of((me[0] ^ m) * rows, rows), rows)


def projection_kernel(marks, block, me, s0, s1, wq, wk, wv, q_gain, k_gain, cosine, signed, *rest):
    q_out, u_out, k_out, kp_out, v_out = rest[-5:]
    rows = s0.shape[0]
    width = wk.shape[1]
    span = jnp.concatenate([s0[...], s1[...]], 0)

    def normed_rotated(u, gain, at):
        inverse = lax.rsqrt(jnp.mean(u * u, -1, keepdims=True) + epsilon)
        a = u * inverse * gain[...]
        return (a * cosine[at, :] + roll_half(a) * signed[at, :]).astype(bf16)

    kv = jnp.dot(span, jnp.concatenate([wk[...], wv[...]], 1), preferred_element_type=f32)
    for n, m in enumerate(marks):
        at = place(me, m, rows)
        here = kv[n * rows : (n + 1) * rows]
        kp_out[at, :] = here[:, :width]
        k_out[at, :] = normed_rotated(here[:, :width], k_gain, at)
        v_out[at, :] = here[:, width:].astype(bf16)

    @pl.loop(0, wq.shape[1] // block)
    def _(step):
        start = pl.multiple_of(step * block, block)
        span = jnp.concatenate([s0[...], s1[...]], 0)
        u = jnp.dot(span, wq[:, pl.ds(start, block)], preferred_element_type=f32)
        for n, m in enumerate(marks):
            at = place(me, m, rows)
            for h in range(block // width):
                part = u[n * rows : (n + 1) * rows, h * width : (h + 1) * width]
                columns = pl.ds(pl.multiple_of(start + h * width, width), width)
                u_out[at, columns] = part
                q_out[at, columns] = normed_rotated(part, q_gain, at)


def projections(me, marks, pair, wq, wk, wv, q_gain, k_gain, cosine, signed, previous):
    rows = pair[0].shape[0]
    length = cosine.shape[0]
    columns, width = wq.shape[1], wk.shape[1]
    inputs = (*pair, wq, wk, wv, q_gain, k_gain, cosine, signed)
    return call(
        functools.partial(projection_kernel, marks, 2 * width),
        (me,),
        (*inputs, *previous),
        [
            ((length, columns), bf16),
            ((length, columns), f32),
            ((length, width), bf16),
            ((length, width), f32),
            ((length, width), bf16),
        ],
        "projections",
        LONG,
        aliases={len(inputs) + n: n for n in range(len(previous))},
    )


class Order:
    def __init__(self, dp, features):
        self.dp = dp
        self.pair = 2 if dp > 2 else 1
        self.halving = [1 << i for i in range(dp.bit_length() - 1) if 1 << i != self.pair]
        self.share = features // dp
        self.group = self.pair * self.share
        self.groups = features // (2 * self.group)
        self.aligned = self.group % 128 == 0 and self.share % 16 == 0

    def rank(self, me, shard):
        result = 0
        for n, bit in enumerate(self.halving):
            same = 1 - (((me ^ shard) // bit) & 1)
            result = result + (same << (len(self.halving) - 1 - n))
        return result

    def wanted(self, me, place):
        target = me & self.pair
        for n, bit in enumerate(self.halving):
            same = (place >> (len(self.halving) - 1 - n)) & 1
            target = target | ((me if same else ~me) & bit)
        return target


def transpose_kernel(order, both, me_dp, *refs):
    count = len(refs) - (2 if both else 1)
    for target in range(2 if both else 1):
        owner = me_dp[0] ^ (order.pair * target)
        side = (owner // order.pair) & 1
        out = refs[count + target]
        for n, source in enumerate(refs[:count]):
            rows = source.shape[0]
            for g in range(order.groups):
                start = pl.multiple_of((2 * g + side) * order.group, order.group)
                turned = source[:, pl.ds(start, order.group)].T
                for low in range(order.pair):
                    shard = (2 * g + side) * order.pair + low
                    at = pl.multiple_of(order.rank(owner, shard) * order.share, order.share)
                    out[pl.ds(at, order.share), n * rows : (n + 1) * rows] = turned[
                        low * order.share : (low + 1) * order.share
                    ]


def transposed(order, me_dp, shards, both, deps=()):
    rows, features = shards[0].shape
    size = (features // 2, rows * len(shards))
    if order.aligned:
        return call(
            functools.partial(transpose_kernel, order, both),
            (me_dp.astype(jnp.int32).reshape(1),),
            shards,
            [(size, bf16)] * (2 if both else 1),
            "transposed",
            1e8,
            deps,
        )
    whole = jnp.concatenate(shards, 0).T.reshape(order.dp, order.share, size[1])
    results = []
    for target in range(2 if both else 1):
        owner = me_dp ^ (order.pair * target)
        results.append(
            jnp.concatenate(
                [
                    lax.dynamic_index_in_dim(whole, order.wanted(owner, i), 0, False)
                    for i in range(order.dp // 2)
                ],
                0,
            )
        )
    return results


def attention_kernel(
    group, block, tile, me, lengths, q, u, k, v, c0, c1, c2, c3, q_gain, cosine, signed, *rest
):
    *sums_in, qg_out, dk_out, dv_out, d_out = rest
    length, width = k.shape
    rows = c0.shape[0]
    base = group * block
    c_base = base % c0.shape[1]
    scale = width ** (-0.5)
    constant = scale * math.log2(math.e)
    valid = lengths[0]
    for m, c in enumerate((c0, c1, c2, c3)):
        at = place(me, m, rows)
        part = c[:, c_base : c_base + block].astype(f32)
        position = lax.broadcasted_iota(jnp.int32, part.shape, 0) + (me[0] ^ m) * rows
        d_out[at, :] = jnp.where(position < valid, part, 0.0).astype(bf16)
    for block_index in range(length // tile):
        here = slice(block_index * tile, (block_index + 1) * tile)
        size = (block_index + 1) * tile
        seen = slice(0, size)
        keys = lax.broadcasted_iota(jnp.int32, (size, tile), 0)
        queries = lax.broadcasted_iota(jnp.int32, (size, tile), 1) + block_index * tile
        allowed = (keys <= queries) & (keys < valid)
        dk_sum = dv_sum = None
        for h in range(block // width):
            part = slice(base + h * width, base + (h + 1) * width)
            local_part = slice(h * width, (h + 1) * width)
            q_head = q[here, part]
            o_grad = d_out[here, local_part]
            scores = lax.dot_general(
                k[seen, :], q_head, (((1,), (1,)), ((), ())), preferred_element_type=f32
            )
            weights = jnp.where(allowed, jnp.exp2(scores * constant), 0.0)
            probs = weights * (1.0 / jnp.sum(weights, 0, keepdims=True))
            low = probs.astype(bf16)
            dprob = lax.dot_general(
                v[seen, :], o_grad, (((1,), (1,)), ((), ())), preferred_element_type=f32
            )
            delta = jnp.sum(low.astype(f32) * dprob, 0, keepdims=True)
            dscore = (probs * (dprob - delta)).astype(bf16)
            dq = lax.dot_general(
                dscore, k[seen, :], (((0,), (0,)), ((), ())), preferred_element_type=f32
            ) * scale
            dk_head = jnp.dot(dscore, q_head, preferred_element_type=f32)
            dv_head = jnp.dot(low, o_grad, preferred_element_type=f32)
            dk_sum = dk_head if dk_sum is None else dk_sum + dk_head
            dv_sum = dv_head if dv_sum is None else dv_sum + dv_head
            back = dq * cosine[here, :] - roll_half(dq) * signed[here, :]
            qg_out[here, local_part] = norm_gradient(u[here, part], q_gain[...], back).astype(bf16)
        for out, total, index in ((dk_out, dk_sum, 0), (dv_out, dv_sum, 1)):
            old = size - tile
            if block_index:
                out[:old, :] += total[:old]
            out[old:size, :] = total[old:]
            if sums_in:
                out[old:size, :] += sums_in[index][old:size, :]


def attention_last_kernel(group, block, tile, *refs):
    *inputs, kp, k_gain, dk_in, dv_in, out, d_out, dk_out, dv_out = refs
    attention_kernel(group, block, tile, *inputs, dk_in, dv_in, out, dk_out, dv_out, d_out)
    cosine, signed = inputs[-2:]
    width = kp.shape[1]
    dk = dk_out[...] * width ** (-0.5)
    back = dk * cosine[...] - roll_half(dk) * signed[...]
    out[:, block : block + width] = norm_gradient(kp[...], k_gain[...], back).astype(bf16)
    out[:, block + width :] = dv_out[...].astype(bf16)


def attention(group, last, block, scalars, inputs, k_inputs, sums, deps, flops):
    length, width = inputs[2].shape
    tile = min(256, length)
    settings = (group, block, tile)
    scratch = [pltpu.VMEM((length, block), bf16)]
    grads = ((length, block), bf16)
    if last:
        return call(
            functools.partial(attention_last_kernel, *settings),
            scalars,
            (*inputs, *k_inputs, *sums),
            [((length, block + 2 * width), bf16)],
            "attention",
            flops,
            deps,
            scratch + [pltpu.VMEM((length, width), f32)] * 2,
        )
    return call(
        functools.partial(attention_kernel, *settings),
        scalars,
        (*inputs, *sums),
        [grads] + [((length, width), f32)] * 2,
        "attention",
        flops,
        deps,
        scratch,
    )


def weight_sums(start, me, transposes, own_g, other_g, send, keep):
    columns = slice(start, start + send.shape[1])
    rows = own_g.shape[0] // 4
    half = send.shape[0]
    rhs = [g[place(me, m, rows), columns] for g in (own_g, other_g) for m in range(4)]
    rhs = jnp.concatenate(rhs, 0)
    for out, at in ((send, 0), (keep, half)):
        lhs = jnp.concatenate([t[at : at + half, :] for t in transposes], 1)
        out[...] = jnp.dot(lhs, rhs, preferred_element_type=f32).astype(out.dtype)


def weight_kernel(start, me, *refs):
    *transposes, own_g, other_g, send, keep = refs
    weight_sums(start, me, transposes, own_g, other_g, send, keep)


def both_kernel(start, count, first, tile, me, *refs):
    transposes, refs = refs[:count], refs[count:]
    own_g, other_g, *parts, wq, wk, wv, send, keep, in_send, in_keep, grads = refs
    weight_sums(start, me, transposes, own_g, other_g, send, keep)
    half = in_send.shape[0]
    rows = half // 2
    block = parts[0].shape[1]
    for n, m in enumerate((3, 1, 2, 0)):
        at = place(me, m, rows)
        for g, ref in enumerate(parts):
            here = slice(g * block, g * block + ref.shape[1])
            grads[n * rows : (n + 1) * rows, here] = ref[at, :]

    @pl.loop(0, in_send.shape[1] // tile)
    def _(step):
        at = pl.ds(pl.multiple_of(first + step * tile, tile), tile)
        to = pl.ds(pl.multiple_of(step * tile, tile), tile)
        weights = jnp.concatenate([wq[at, :], wk[at, :], wv[at, :]], 1)
        total = lax.dot_general(
            grads[...], weights, (((1,), (1,)), ((), ())), preferred_element_type=f32
        )
        in_send[:, to] = total[:half].astype(bf16)
        in_keep[:, to] = total[half:]


def weight_products(me, transposes, start, columns, own_g, other_g, deps, flops, extra=None):
    half = transposes[0].shape[0] // 2
    length = own_g.shape[0]
    outputs = [((half, columns), bf16), ((half, columns), f32)]
    inputs = (*transposes, own_g, other_g)
    if extra is None:
        kernel = functools.partial(weight_kernel, start)
        return call(kernel, (me,), inputs, outputs, "weight_products", flops, deps)
    (first, count), parts, weights = extra
    tile = 256 if count % 256 == 0 else count
    return call(
        functools.partial(both_kernel, start, len(transposes), first, tile),
        (me,),
        (*inputs, *parts, *weights),
        outputs + [((length // 2, count), bf16), ((length // 2, count), f32)],
        "both_products",
        flops,
        deps,
        [pltpu.VMEM((length, sum(p.shape[1] for p in parts)), bf16)],
        limit=16,
    )


def halve_kernel(keep, received, send, rest):
    half = send.shape[0]
    send[...] = (keep[:half] + received[:half].astype(f32)).astype(bf16)
    rest[...] = keep[half:] + received[half:].astype(f32)


def halve(keep, received, deps=()):
    rows, columns = keep.shape
    half = rows // 2
    if half % 16:
        total = keep + received.astype(f32)
        return total[:half].astype(bf16), total[half:]
    size = (half, columns)
    return call(halve_kernel, (), (keep, received), [(size, bf16), (size, f32)], "halve", 2e9, deps)


def input_sum_kernel(*refs):
    *inputs, out, token = refs
    count = len(inputs) // 2
    columns = inputs[0].shape[1]
    for n in range(count):
        total = inputs[n][...] + inputs[count + n][...].astype(f32)
        out[:, n * columns : (n + 1) * columns] = total.astype(bf16)
    token[...] = jnp.zeros_like(token)


def query_sum_kernel(first, *refs):
    *inputs, out, token = refs[first:]
    count = len(inputs) // 2
    columns = inputs[0].shape[1]
    for n in range(count):
        total = inputs[n][...] + inputs[count + n][...].astype(f32)
        out[:, n * columns : (n + 1) * columns] = total
    token[...] = jnp.zeros_like(token)


def pair_sum_kernel(first, *refs):
    kept, received, key_out, value_out = refs[first:]
    width = key_out.shape[1]
    total = kept[...] + received[...].astype(f32)
    key_out[...] = total[:, :width]
    value_out[...] = total[:, width:]


def last_sum(kernel, deps, inputs, outputs):
    return pl.pallas_call(
        functools.partial(kernel, len(deps)) if deps else kernel,
        in_specs=[ANY] * len(deps) + [VMEM] * len(inputs),
        out_shape=[jax.ShapeDtypeStruct(shape, dtype) for shape, dtype in outputs],
        compiler_params=pltpu.CompilerParams(vmem_limit_bytes=14 * MIB),
        cost_estimate=pl.CostEstimate(flops=1024, bytes_accessed=1024, transcendentals=0),
        name="last_sum",
    )(*deps, *inputs)


def local(dp, sp, normed, wq, wk, wv, q_gain, k_gain, ctx_grad, lengths):
    rows, features = normed.shape
    width = q_gain.shape[0]
    columns = wq.shape[1]
    length = rows * sp
    block = 2 * width
    groups = columns // block
    me_sp = lax.axis_index("sp")
    me_dp = lax.axis_index("dp")
    me = me_sp.astype(jnp.int32).reshape(1)
    q_gain = q_gain.reshape(1, width)
    k_gain = k_gain.reshape(1, width)
    cosine, signed = angle_tables(length, width)
    over_sp = functools.partial(exchange, axis="sp", size=sp)
    over_dp = functools.partial(exchange, axis="dp", size=dp)
    order = Order(dp, features)

    def cotangent(m, part):
        size = columns // 2
        return lax.dynamic_slice_in_dim(ctx_grad, (me_sp ^ m) * columns + part * size, size, 1)

    far = over_sp(normed, bit=2)
    near = over_sp(normed, bit=1)

    own_o, pair_o = transposed(order, me_dp, (normed,), True)
    other_o = over_dp(pair_o, bit=order.pair)
    (own_n,) = transposed(order, me_dp, (near,), False)
    previous = projections(
        me, (0, 1), (normed, near), wq, wk, wv, q_gain, k_gain, cosine, signed, ()
    )
    cots = [cotangent(m, part) for part in range(2) for m in range(4)]
    far, other_o, own_n, *rest = lax.optimization_barrier((far, other_o, own_n, *previous, *cots))
    previous, cots = rest[: len(previous)], rest[len(previous) :]

    diagonal = over_sp(far, bit=1)
    cs = [
        (cots[4 * part],) + tuple(over_sp(cots[4 * part + m], bit=m) for m in (1, 2, 3))
        for part in range(2)
    ]
    own_f, pair_f = transposed(order, me_dp, (far,), True)
    other_f = over_dp(pair_f, bit=order.pair)
    q, u, k, kp, v = projections(
        me, (2, 3), (far, diagonal), wq, wk, wv, q_gain, k_gain, cosine, signed, previous
    )
    (own_d,) = transposed(order, me_dp, (diagonal,), False, (k, *cs[0][2:]))

    parts, received, firsts = [], [], []
    sums = ()

    def heads(g, deps, flops):
        inputs = (q, u, k, v, *cs[2 * g // groups], q_gain, cosine, signed)
        result = attention(
            g, g == groups - 1, block, (me, lengths), inputs, (kp, k_gain), sums, deps, flops
        )
        parts.append(result[0])
        received.append(over_dp(result[0], bit=order.pair))
        return result[1:]

    def product(n, deps, flops, extra=None):
        send, keep, *more = weight_products(
            me, (own_o, own_n, own_f, own_d, other_o, other_n, other_f, other_d), max(n - groups + 1, 0) * block, block,
            parts[min(n, groups - 1)], received[min(n, groups - 1)], deps, flops, extra,
        )
        firsts.append((keep, over_dp(send, bit=order.halving[0])))
        return (keep, *more)

    def input_part(n):
        return ((n * features // 2, features // 2), parts, (wq, wk, wv))

    def halved(sent, kept, deps=()):
        sent, kept = halve(kept, over_sp(sent, bit=1), deps)
        return kept, over_sp(sent, bit=2)

    def last_steps(keep, came, deps=()):
        for bit in order.halving[1:]:
            send, keep = halve(keep, came, deps)
            came = over_dp(send, bit=bit)
        return keep, came

    sums = heads(0, (own_d,), SHORT)
    other_o, other_f, tied = lax.optimization_barrier((other_o, other_f, sums[0]))
    sums = (tied, sums[1])
    other_n, other_d = over_sp(other_o, bit=1), over_sp(other_f, bit=1)
    sums = heads(1, (), LONG)
    sums = heads(2, (received[0],), LONG)
    keep, = product(0, (sums[0],), SHORT)
    heads(3, (keep, received[1]), LONG)
    keep, = product(1, (parts[3],), SHORT)
    ends = [last_steps(*firsts[0])]
    keep, *first_half = product(2, (keep, ends[0][0]), LONG, input_part(0))
    ends.append(last_steps(*firsts[1]))
    keep, *second_half = product(3, (keep, ends[1][0], ends[0][1]), LONG, input_part(1))
    ends.append(last_steps(*firsts[2]))
    tied = product(4, (keep, ends[2][0], ), LONG)
    inputs = [halved(*half, (tied[0],)) for half in (first_half, second_half)]
    ends.append(last_steps(*firsts[3], (ends[1][1],)))
    ends.append(last_steps(*firsts[4], (ends[2][1],)))
    pieces = [i[0] for i in inputs] + [i[1] for i in inputs]
    token = ((8, 128), f32)
    input_gradient, order_mark = last_sum(
        input_sum_kernel, (), pieces, [((rows, features), bf16), token]
    )
    pieces = [end[0] for end in ends[:-1]] + [end[1] for end in ends[:-1]]
    grad_query, order_mark = last_sum(
        query_sum_kernel, (order_mark,), pieces, [((order.share, columns), f32), token]
    )
    grad_key, grad_value = last_sum(
        pair_sum_kernel, (order_mark,), ends[-1], [((order.share, width), f32)] * 2
    )
    return input_gradient, grad_query, grad_key, grad_value


def solution(mesh):
    in_specs = (
        P(("dp", "sp"), None),
        P(None, "sp"),
        P(None, "sp"),
        P(None, "sp"),
        P(),
        P(),
        P(("dp", "sp"), None),
        P("dp"),
    )
    out_specs = (P(("dp", "sp"), None), P("dp", "sp"), P("dp", "sp"), P("dp", "sp"))
    body = functools.partial(local, mesh.shape["dp"], mesh.shape["sp"])
    return jax.shard_map(body, mesh=mesh, in_specs=in_specs, out_specs=out_specs, check_vma=False)
```

```python
import functools
import math

import jax
import jax.numpy as jnp
from jax import lax
from jax.experimental import pallas as pl
from jax.experimental.pallas import tpu as pltpu
from jax.sharding import PartitionSpec as P

epsilon = 1e-06
log_base = math.log(1000000.0)
bf16 = jnp.bfloat16
f32 = jnp.float32
MIB = 1024 * 1024
LONG = 2.3e10
SHORT = 1e6
SMEM = pl.BlockSpec(memory_space=pltpu.SMEM)
VMEM = pl.BlockSpec(memory_space=pltpu.VMEM)
ANY = pl.BlockSpec(memory_space=pl.ANY)


def call(kernel, scalars, inputs, outputs, name, flops, deps=(), scratch=(), aliases=None, limit=14):
    count = len(deps)

    def body(*refs):
        return kernel(*refs[count:])

    return pl.pallas_call(
        body,
        in_specs=[ANY] * count + [SMEM] * len(scalars) + [VMEM] * len(inputs),
        out_specs=[VMEM] * len(outputs),
        out_shape=[jax.ShapeDtypeStruct(shape, dtype) for shape, dtype in outputs],
        scratch_shapes=list(scratch),
        input_output_aliases={
            count + len(scalars) + i: o for i, o in (aliases or {}).items()
        },
        compiler_params=pltpu.CompilerParams(vmem_limit_bytes=limit * MIB),
        cost_estimate=pl.CostEstimate(
            flops=int(flops), bytes_accessed=1024, transcendentals=0
        ),
        name=name,
    )(*deps, *scalars, *inputs)


def angle_tables(length, width):
    position = jnp.arange(length, dtype=jnp.int32).astype(f32)
    freqs = jnp.exp(jnp.arange(width // 2, dtype=f32) * (-2.0 * log_base / width))
    angles = position[:, None] * freqs[None, :]
    cosine = jnp.cos(angles)
    sine = jnp.sin(angles)
    return jnp.concatenate([cosine, cosine], 1), jnp.concatenate([-sine, sine], 1)


def exchange(value, axis, size, bit):
    return lax.ppermute(value, axis, [(d, d ^ bit) for d in range(size)])


def roll_half(a):
    return pltpu.roll(a, a.shape[-1] // 2, a.ndim - 1)


def norm_gradient(values, gain, grads):
    inverse = lax.rsqrt(jnp.mean(values * values, -1, keepdims=True) + epsilon)
    weighted = gain * grads
    mean = jnp.mean(values * weighted, -1, keepdims=True)
    return inverse * weighted - values * (inverse * inverse * inverse * mean)


def place(me, m, rows):
    return pl.ds(pl.multiple_of((me[0] ^ m) * rows, rows), rows)


def projection_kernel(marks, block, me, s0, s1, wq, wk, wv, q_gain, k_gain, cosine, signed, *rest):
    q_out, u_out, k_out, kp_out, v_out = rest[-5:]
    rows = s0.shape[0]
    width = wk.shape[1]
    span = jnp.concatenate([s0[...], s1[...]], 0)

    def normed_rotated(u, gain, at):
        inverse = lax.rsqrt(jnp.mean(u * u, -1, keepdims=True) + epsilon)
        a = u * inverse * gain[...]
        return (a * cosine[at, :] + roll_half(a) * signed[at, :]).astype(bf16)

    kv = jnp.dot(span, jnp.concatenate([wk[...], wv[...]], 1), preferred_element_type=f32)
    for n, m in enumerate(marks):
        at = place(me, m, rows)
        here = kv[n * rows : (n + 1) * rows]
        kp_out[at, :] = here[:, :width]
        k_out[at, :] = normed_rotated(here[:, :width], k_gain, at)
        v_out[at, :] = here[:, width:].astype(bf16)

    @pl.loop(0, wq.shape[1] // block)
    def _(step):
        start = pl.multiple_of(step * block, block)
        span = jnp.concatenate([s0[...], s1[...]], 0)
        u = jnp.dot(span, wq[:, pl.ds(start, block)], preferred_element_type=f32)
        for n, m in enumerate(marks):
            at = place(me, m, rows)
            for h in range(block // width):
                part = u[n * rows : (n + 1) * rows, h * width : (h + 1) * width]
                columns = pl.ds(pl.multiple_of(start + h * width, width), width)
                u_out[at, columns] = part
                q_out[at, columns] = normed_rotated(part, q_gain, at)


def projections(me, marks, pair, wq, wk, wv, q_gain, k_gain, cosine, signed, previous):
    rows = pair[0].shape[0]
    length = cosine.shape[0]
    columns, width = wq.shape[1], wk.shape[1]
    inputs = (*pair, wq, wk, wv, q_gain, k_gain, cosine, signed)
    return call(
        functools.partial(projection_kernel, marks, 2 * width),
        (me,),
        (*inputs, *previous),
        [
            ((length, columns), bf16),
            ((length, columns), f32),
            ((length, width), bf16),
            ((length, width), f32),
            ((length, width), bf16),
        ],
        "projections",
        LONG,
        aliases={len(inputs) + n: n for n in range(len(previous))},
    )


class Order:
    def __init__(self, dp, features):
        self.dp = dp
        self.pair = 2 if dp > 2 else 1
        self.halving = [1 << i for i in range(dp.bit_length() - 1) if 1 << i != self.pair]
        self.share = features // dp
        self.group = self.pair * self.share
        self.groups = features // (2 * self.group)
        self.aligned = self.group % 128 == 0 and self.share % 16 == 0

    def rank(self, me, shard):
        result = 0
        for n, bit in enumerate(self.halving):
            same = 1 - (((me ^ shard) // bit) & 1)
            result = result + (same << (len(self.halving) - 1 - n))
        return result

    def wanted(self, me, place):
        target = me & self.pair
        for n, bit in enumerate(self.halving):
            same = (place >> (len(self.halving) - 1 - n)) & 1
            target = target | ((me if same else ~me) & bit)
        return target


def transpose_kernel(order, both, me_dp, *refs):
    count = len(refs) - (2 if both else 1)
    for target in range(2 if both else 1):
        owner = me_dp[0] ^ (order.pair * target)
        side = (owner // order.pair) & 1
        out = refs[count + target]
        for n, source in enumerate(refs[:count]):
            rows = source.shape[0]
            for g in range(order.groups):
                start = pl.multiple_of((2 * g + side) * order.group, order.group)
                turned = source[:, pl.ds(start, order.group)].T
                for low in range(order.pair):
                    shard = (2 * g + side) * order.pair + low
                    at = pl.multiple_of(order.rank(owner, shard) * order.share, order.share)
                    out[pl.ds(at, order.share), n * rows : (n + 1) * rows] = turned[
                        low * order.share : (low + 1) * order.share
                    ]


def transposed(order, me_dp, shards, both, deps=()):
    rows, features = shards[0].shape
    size = (features // 2, rows * len(shards))
    if order.aligned:
        return call(
            functools.partial(transpose_kernel, order, both),
            (me_dp.astype(jnp.int32).reshape(1),),
            shards,
            [(size, bf16)] * (2 if both else 1),
            "transposed",
            1e8,
            deps,
        )
    whole = jnp.concatenate(shards, 0).T.reshape(order.dp, order.share, size[1])
    results = []
    for target in range(2 if both else 1):
        owner = me_dp ^ (order.pair * target)
        results.append(
            jnp.concatenate(
                [
                    lax.dynamic_index_in_dim(whole, order.wanted(owner, i), 0, False)
                    for i in range(order.dp // 2)
                ],
                0,
            )
        )
    return results


def attention_kernel(
    group, block, tile, me, lengths, q, u, k, v, c0, c1, c2, c3, q_gain, cosine, signed, *rest
):
    *sums_in, qg_out, dk_out, dv_out, d_out = rest
    length, width = k.shape
    rows = c0.shape[0]
    base = group * block
    c_base = base % c0.shape[1]
    scale = width ** (-0.5)
    constant = scale * math.log2(math.e)
    valid = lengths[0]
    for m, c in enumerate((c0, c1, c2, c3)):
        at = place(me, m, rows)
        part = c[:, c_base : c_base + block].astype(f32)
        position = lax.broadcasted_iota(jnp.int32, part.shape, 0) + (me[0] ^ m) * rows
        d_out[at, :] = jnp.where(position < valid, part, 0.0).astype(bf16)
    for block_index in range(length // tile):
        here = slice(block_index * tile, (block_index + 1) * tile)
        size = (block_index + 1) * tile
        seen = slice(0, size)
        keys = lax.broadcasted_iota(jnp.int32, (size, tile), 0)
        queries = lax.broadcasted_iota(jnp.int32, (size, tile), 1) + block_index * tile
        allowed = (keys <= queries) & (keys < valid)
        dk_sum = dv_sum = None
        for h in range(block // width):
            part = slice(base + h * width, base + (h + 1) * width)
            local_part = slice(h * width, (h + 1) * width)
            q_head = q[here, part]
            o_grad = d_out[here, local_part]
            scores = lax.dot_general(
                k[seen, :], q_head, (((1,), (1,)), ((), ())), preferred_element_type=f32
            )
            weights = jnp.where(allowed, jnp.exp2(scores * constant), 0.0)
            probs = weights * (1.0 / jnp.sum(weights, 0, keepdims=True))
            low = probs.astype(bf16)
            dprob = lax.dot_general(
                v[seen, :], o_grad, (((1,), (1,)), ((), ())), preferred_element_type=f32
            )
            delta = jnp.sum(low.astype(f32) * dprob, 0, keepdims=True)
            dscore = (probs * (dprob - delta)).astype(bf16)
            dq = lax.dot_general(
                dscore, k[seen, :], (((0,), (0,)), ((), ())), preferred_element_type=f32
            ) * scale
            dk_head = jnp.dot(dscore, q_head, preferred_element_type=f32)
            dv_head = jnp.dot(low, o_grad, preferred_element_type=f32)
            dk_sum = dk_head if dk_sum is None else dk_sum + dk_head
            dv_sum = dv_head if dv_sum is None else dv_sum + dv_head
            back = dq * cosine[here, :] - roll_half(dq) * signed[here, :]
            qg_out[here, local_part] = norm_gradient(u[here, part], q_gain[...], back).astype(bf16)
        for out, total, index in ((dk_out, dk_sum, 0), (dv_out, dv_sum, 1)):
            old = size - tile
            if block_index:
                out[:old, :] += total[:old]
            out[old:size, :] = total[old:]
            if sums_in:
                out[old:size, :] += sums_in[index][old:size, :]


def attention_last_kernel(group, block, tile, *refs):
    *inputs, kp, k_gain, dk_in, dv_in, out, d_out, dk_out, dv_out = refs
    attention_kernel(group, block, tile, *inputs, dk_in, dv_in, out, dk_out, dv_out, d_out)
    cosine, signed = inputs[-2:]
    width = kp.shape[1]
    dk = dk_out[...] * width ** (-0.5)
    back = dk * cosine[...] - roll_half(dk) * signed[...]
    out[:, block : block + width] = norm_gradient(kp[...], k_gain[...], back).astype(bf16)
    out[:, block + width :] = dv_out[...].astype(bf16)


def attention(group, last, block, scalars, inputs, k_inputs, sums, deps, flops):
    length, width = inputs[2].shape
    tile = min(256, length)
    settings = (group, block, tile)
    scratch = [pltpu.VMEM((length, block), bf16)]
    grads = ((length, block), bf16)
    if last:
        return call(
            functools.partial(attention_last_kernel, *settings),
            scalars,
            (*inputs, *k_inputs, *sums),
            [((length, block + 2 * width), bf16)],
            "attention",
            flops,
            deps,
            scratch + [pltpu.VMEM((length, width), f32)] * 2,
        )
    return call(
        functools.partial(attention_kernel, *settings),
        scalars,
        (*inputs, *sums),
        [grads] + [((length, width), f32)] * 2,
        "attention",
        flops,
        deps,
        scratch,
    )


def weight_sums(start, me, transposes, own_g, other_g, send, keep):
    columns = slice(start, start + send.shape[1])
    rows = own_g.shape[0] // 4
    half = send.shape[0]
    rhs = [g[place(me, m, rows), columns] for g in (own_g, other_g) for m in range(4)]
    rhs = jnp.concatenate(rhs, 0)
    for out, at in ((send, 0), (keep, half)):
        lhs = jnp.concatenate([t[at : at + half, :] for t in transposes], 1)
        out[...] = jnp.dot(lhs, rhs, preferred_element_type=f32).astype(out.dtype)


def weight_kernel(start, me, *refs):
    *transposes, own_g, other_g, send, keep = refs
    weight_sums(start, me, transposes, own_g, other_g, send, keep)


def both_kernel(start, count, first, tile, me, *refs):
    transposes, refs = refs[:count], refs[count:]
    own_g, other_g, *parts, wq, wk, wv, send, keep, in_send, in_keep, grads = refs
    weight_sums(start, me, transposes, own_g, other_g, send, keep)
    half = in_send.shape[0]
    rows = half // 2
    block = parts[0].shape[1]
    for n, m in enumerate((3, 1, 2, 0)):
        at = place(me, m, rows)
        for g, ref in enumerate(parts):
            here = slice(g * block, g * block + ref.shape[1])
            grads[n * rows : (n + 1) * rows, here] = ref[at, :]

    @pl.loop(0, in_send.shape[1] // tile)
    def _(step):
        at = pl.ds(pl.multiple_of(first + step * tile, tile), tile)
        to = pl.ds(pl.multiple_of(step * tile, tile), tile)
        weights = jnp.concatenate([wq[at, :], wk[at, :], wv[at, :]], 1)
        total = lax.dot_general(
            grads[...], weights, (((1,), (1,)), ((), ())), preferred_element_type=f32
        )
        in_send[:, to] = total[:half].astype(bf16)
        in_keep[:, to] = total[half:]


def weight_products(me, transposes, start, columns, own_g, other_g, deps, flops, extra=None):
    half = transposes[0].shape[0] // 2
    length = own_g.shape[0]
    outputs = [((half, columns), bf16), ((half, columns), f32)]
    inputs = (*transposes, own_g, other_g)
    if extra is None:
        kernel = functools.partial(weight_kernel, start)
        return call(kernel, (me,), inputs, outputs, "weight_products", flops, deps)
    (first, count), parts, weights = extra
    tile = 256 if count % 256 == 0 else count
    return call(
        functools.partial(both_kernel, start, len(transposes), first, tile),
        (me,),
        (*inputs, *parts, *weights),
        outputs + [((length // 2, count), bf16), ((length // 2, count), f32)],
        "both_products",
        flops,
        deps,
        [pltpu.VMEM((length, sum(p.shape[1] for p in parts)), bf16)],
        limit=16,
    )


def halve_kernel(keep, received, send, rest):
    half = send.shape[0]
    send[...] = (keep[:half] + received[:half].astype(f32)).astype(bf16)
    rest[...] = keep[half:] + received[half:].astype(f32)


def halve(keep, received, deps=()):
    rows, columns = keep.shape
    half = rows // 2
    if half % 16:
        total = keep + received.astype(f32)
        return total[:half].astype(bf16), total[half:]
    size = (half, columns)
    return call(halve_kernel, (), (keep, received), [(size, bf16), (size, f32)], "halve", 2e9, deps)


def input_sum_kernel(*refs):
    *inputs, out, token = refs
    count = len(inputs) // 2
    columns = inputs[0].shape[1]
    for n in range(count):
        total = inputs[n][...] + inputs[count + n][...].astype(f32)
        out[:, n * columns : (n + 1) * columns] = total.astype(bf16)
    token[...] = jnp.zeros_like(token)


def query_sum_kernel(first, *refs):
    *inputs, out, token = refs[first:]
    count = len(inputs) // 2
    columns = inputs[0].shape[1]
    for n in range(count):
        total = inputs[n][...] + inputs[count + n][...].astype(f32)
        out[:, n * columns : (n + 1) * columns] = total
    token[...] = jnp.zeros_like(token)


def pair_sum_kernel(first, *refs):
    kept, received, key_out, value_out = refs[first:]
    width = key_out.shape[1]
    total = kept[...] + received[...].astype(f32)
    key_out[...] = total[:, :width]
    value_out[...] = total[:, width:]


def last_sum(kernel, deps, inputs, outputs):
    return pl.pallas_call(
        functools.partial(kernel, len(deps)) if deps else kernel,
        in_specs=[ANY] * len(deps) + [VMEM] * len(inputs),
        out_shape=[jax.ShapeDtypeStruct(shape, dtype) for shape, dtype in outputs],
        compiler_params=pltpu.CompilerParams(vmem_limit_bytes=14 * MIB),
        cost_estimate=pl.CostEstimate(flops=1024, bytes_accessed=1024, transcendentals=0),
        name="last_sum",
    )(*deps, *inputs)


def local(dp, sp, normed, wq, wk, wv, q_gain, k_gain, ctx_grad, lengths):
    rows, features = normed.shape
    width = q_gain.shape[0]
    columns = wq.shape[1]
    length = rows * sp
    block = 2 * width
    groups = columns // block
    me_sp = lax.axis_index("sp")
    me_dp = lax.axis_index("dp")
    me = me_sp.astype(jnp.int32).reshape(1)
    q_gain = q_gain.reshape(1, width)
    k_gain = k_gain.reshape(1, width)
    cosine, signed = angle_tables(length, width)
    over_sp = functools.partial(exchange, axis="sp", size=sp)
    over_dp = functools.partial(exchange, axis="dp", size=dp)
    order = Order(dp, features)

    def cotangent(m, part):
        size = columns // 2
        return lax.dynamic_slice_in_dim(ctx_grad, (me_sp ^ m) * columns + part * size, size, 1)

    far = over_sp(normed, bit=2)
    near = over_sp(normed, bit=1)

    own_o, pair_o = transposed(order, me_dp, (normed,), True)
    other_o = over_dp(pair_o, bit=order.pair)
    (own_n,) = transposed(order, me_dp, (near,), False)
    previous = projections(
        me, (0, 1), (normed, near), wq, wk, wv, q_gain, k_gain, cosine, signed, ()
    )
    cots = [cotangent(m, part) for part in range(2) for m in range(4)]
    far, other_o, own_n, *rest = lax.optimization_barrier((far, other_o, own_n, *previous, *cots))
    previous, cots = rest[: len(previous)], rest[len(previous) :]

    diagonal = over_sp(far, bit=1)
    cs = [
        (cots[4 * part],) + tuple(over_sp(cots[4 * part + m], bit=m) for m in (1, 2, 3))
        for part in range(2)
    ]
    own_f, pair_f = transposed(order, me_dp, (far,), True)
    other_f = over_dp(pair_f, bit=order.pair)
    q, u, k, kp, v = projections(
        me, (2, 3), (far, diagonal), wq, wk, wv, q_gain, k_gain, cosine, signed, previous
    )
    (own_d,) = transposed(order, me_dp, (diagonal,), False, (k, *cs[0][2:]))

    parts, received, firsts = [], [], []
    sums = ()

    def heads(g, deps, flops):
        inputs = (q, u, k, v, *cs[2 * g // groups], q_gain, cosine, signed)
        result = attention(
            g, g == groups - 1, block, (me, lengths), inputs, (kp, k_gain), sums, deps, flops
        )
        parts.append(result[0])
        received.append(over_dp(result[0], bit=order.pair))
        return result[1:]

    def product(n, deps, flops, extra=None):
        send, keep, *more = weight_products(
            me, (own_o, own_n, own_f, own_d, other_o, other_n, other_f, other_d), max(n - groups + 1, 0) * block, block,
            parts[min(n, groups - 1)], received[min(n, groups - 1)], deps, flops, extra,
        )
        firsts.append((keep, over_dp(send, bit=order.halving[0])))
        return (keep, *more)

    def input_part(n):
        return ((n * features // 2, features // 2), parts, (wq, wk, wv))

    def halved(sent, kept, deps=()):
        sent, kept = halve(kept, over_sp(sent, bit=1), deps)
        return kept, over_sp(sent, bit=2)

    def last_steps(keep, came, deps=()):
        for bit in order.halving[1:]:
            send, keep = halve(keep, came, deps)
            came = over_dp(send, bit=bit)
        return keep, came

    sums = heads(0, (own_d,), SHORT)
    other_o, other_f, tied = lax.optimization_barrier((other_o, other_f, sums[0]))
    sums = (tied, sums[1])
    other_n, other_d = over_sp(other_o, bit=1), over_sp(other_f, bit=1)
    sums = heads(1, (), LONG)
    sums = heads(2, (received[0],), LONG)
    keep, = product(0, (sums[0],), SHORT)
    heads(3, (keep, received[1]), LONG)
    keep, = product(1, (parts[3],), SHORT)
    ends = [last_steps(*firsts[0])]
    keep, *first_half = product(2, (keep, ends[0][0]), LONG, input_part(0))
    ends.append(last_steps(*firsts[1]))
    keep, *second_half = product(3, (keep, ends[1][0], ends[0][1]), LONG, input_part(1))
    ends.append(last_steps(*firsts[2]))
    tied = product(4, (keep, ends[2][0], ends[1][1]), LONG)
    inputs = [halved(*half, (tied[0],)) for half in (first_half, second_half)]
    ends.append(last_steps(*firsts[3], (inputs[0][0], inputs[1][0], )))
    ends.append(last_steps(*firsts[4], (ends[2][1],)))
    pieces = [i[0] for i in inputs] + [i[1] for i in inputs]
    token = ((8, 128), f32)
    input_gradient, order_mark = last_sum(
        input_sum_kernel, (), pieces, [((rows, features), bf16), token]
    )
    pieces = [end[0] for end in ends[:-1]] + [end[1] for end in ends[:-1]]
    grad_query, order_mark = last_sum(
        query_sum_kernel, (order_mark,), pieces, [((order.share, columns), f32), token]
    )
    grad_key, grad_value = last_sum(
        pair_sum_kernel, (order_mark,), ends[-1], [((order.share, width), f32)] * 2
    )
    return input_gradient, grad_query, grad_key, grad_value


def solution(mesh):
    in_specs = (
        P(("dp", "sp"), None),
        P(None, "sp"),
        P(None, "sp"),
        P(None, "sp"),
        P(),
        P(),
        P(("dp", "sp"), None),
        P("dp"),
    )
    out_specs = (P(("dp", "sp"), None), P("dp", "sp"), P("dp", "sp"), P("dp", "sp"))
    body = functools.partial(local, mesh.shape["dp"], mesh.shape["sp"])
    return jax.shard_map(body, mesh=mesh, in_specs=in_specs, out_specs=out_specs, check_vma=False)
```
